32 devices in a mesh: seq: 8 (over z, core), rep: 4 (over y, x).
Axes of the slice: x: 2, y: 2, z: 4, core: 2. Of those that a mesh axis runs over, the one named last changes fastest.
Arguments:
- probe_vectors: bfloat16 [4, 1024, 1024], P('rep', 'seq'), may hold values from -200 to 200
- lookup_vectors: bfloat16 [4, 1024, 1024], P('rep', 'seq'), may hold values from -9 to 9
- content_vectors: bfloat16 [4, 1024, 1024], P('rep', 'seq'), may hold values from -6 to 6
- recursion_levels: int32 [4, 1024], P('rep', 'seq'), may hold values from 1 to 3, as said below
- routing_preactivations: float32 [4, 1024], P('rep', 'seq'), may hold values from -6 to 6
- attender_multiplier: float32 [8], replicated, may hold values from 0.5 to 2
- upstream_adjoint: bfloat16 [4, 256, 1024], P('rep', 'seq'), may hold values from -20 to 20
Outputs:
- mixed_rows: bfloat16 [4, 256, 1024], P('rep', 'seq')
- gate_grad: float32 [4, 256], P('rep', 'seq')
- query_grad: bfloat16 [4, 256, 1024], P('rep', 'seq')
- key_grad: bfloat16 [4, 256, 1024], P('rep', 'seq')
- value_grad: bfloat16 [4, 256, 1024], P('rep', 'seq')
- attender_multiplier_derivative: float32 [8], P('seq')
The draws below stay inside these ranges and needn't reach their ends.
Inputs may be any that keep to these rules, and one draw needn't show every extreme that they name: `recursion_levels`: in each block of 128 tokens at least one and at most 32 tokens have depths over 2; in every draw some block has exactly 32.
All inputs are finite; a program needn't handle non-finite values.
Results may differ from the reference program's by a relative error of at most 0.0058.
Values may be sent and summed in bfloat16 or wider, within the bound.
A program may use at most 64 MiB of HBM per device.

```python
import math
import jax
import jax.numpy as jnp
from jax import lax

TOK_DEV = 128
HDIM = 128
STEP = 2
ATTENDER_AMOUNT = 8
D = 1024
CAP = 32
LEN = 1024
ACT = 256
SEQUENCE_AMOUNT = 4
N_SEQ = 8


def shared_rows(key):
    return jnp.clip(jax.random.normal(key, (SEQUENCE_AMOUNT, LEN, D), jnp.float32), -6.0, 6.0)


def draw_lookup_vectors(key, part):
    base = shared_rows(key)
    return base.astype(jnp.bfloat16)


def draw_probe_vectors(key, part):
    key = jax.random.fold_in(key, 5)
    fresh = jnp.clip(jax.random.normal(key, (SEQUENCE_AMOUNT, LEN, D), jnp.float32), -6.0, 6.0)
    return fresh.astype(jnp.bfloat16)


def one_permutation(part_key):
    return jax.random.permutation(part_key, TOK_DEV)


def draw_recursion_levels(key, part):
    key = jax.random.fold_in(key, 7)
    block_count = SEQUENCE_AMOUNT * (LEN // TOK_DEV)
    split_keys = jax.random.split(key, 4)
    lowest = max(1, CAP // 4)
    counts = jax.random.randint(split_keys[0], (block_count,), lowest, CAP + 1)
    chosen = jax.random.randint(split_keys[1], (), 0, block_count)
    counts = jnp.where(jnp.arange(block_count) == chosen, CAP, counts)
    orders = jax.vmap(one_permutation)(jax.random.split(split_keys[2], block_count))
    shallow = jax.random.randint(split_keys[3], (block_count, TOK_DEV), 1, 3)
    deepest = jnp.where(orders < counts[:, None], 3, shallow)
    return deepest.reshape(SEQUENCE_AMOUNT, LEN).astype(jnp.int32)


def draw_upstream_adjoint(key, part):
    key = jax.random.fold_in(key, 9)
    first = jax.random.fold_in(key, 0)
    rising = 0.5 * (1.0 + 2.0 * jnp.arange(SEQUENCE_AMOUNT, dtype=jnp.float32) / max(SEQUENCE_AMOUNT - 1, 1))
    noise = jnp.clip(jax.random.normal(first, (SEQUENCE_AMOUNT, ACT, D), jnp.float32), -6.0, 6.0)
    return (noise * rising[:, None, None]).astype(jnp.bfloat16)


def block_scale(own_key, dims, shards, least, high):
    gain, own = 1.0, jax.random.fold_in(own_key, 6)
    for dim, shards_of in shards:
        heights = jnp.exp(jax.random.uniform(jax.random.fold_in(own, dim), (shards_of,), jnp.float32, least / len(shards), high / len(shards)))
        gain = gain * jnp.repeat(heights, dims[dim] // shards_of).reshape([-1 if axis == dim else 1 for axis in range(len(dims))])
    return gain


def normal_values(own_key, shape, deviation, most, pieces=(), kind=jnp.bfloat16):
    factor_of = block_scale(own_key, shape, pieces, -0.22, 0.18) if pieces else 1.0
    values = jax.random.normal(own_key, shape, jnp.float32) * deviation * factor_of
    return jnp.minimum(jnp.maximum(values, -most), most).astype(kind)


def setup_inputs(seed: int = 0) -> dict:
    key_list = jax.random.split(jax.random.key(seed), 8)
    probe_vectors = draw_probe_vectors(jax.random.fold_in(key_list[7], 71), 0)
    lookup_vectors = draw_lookup_vectors(jax.random.fold_in(key_list[7], 71), 0)
    content_vectors = normal_values(key_list[2], (SEQUENCE_AMOUNT, LEN, D), 1.0, 6.0, ((0, 4), (1, 8)))
    recursion_levels = draw_recursion_levels(jax.random.fold_in(key_list[7], 71), 0)
    routing_preactivations = normal_values(key_list[4], (SEQUENCE_AMOUNT, LEN), 1.5, 6.0, ((0, 4), (1, 8)), jnp.float32)
    attender_multiplier = jnp.clip(jnp.exp(jax.random.uniform(key_list[5], (ATTENDER_AMOUNT,), jnp.float32, math.log(0.5), math.log(2.0))), 0.5, 2.0)
    upstream_adjoint = draw_upstream_adjoint(jax.random.fold_in(key_list[7], 71), 0)
    return dict(probe_vectors=probe_vectors, lookup_vectors=lookup_vectors, content_vectors=content_vectors, recursion_levels=recursion_levels, routing_preactivations=routing_preactivations, attender_multiplier=attender_multiplier, upstream_adjoint=upstream_adjoint)


def compact_index(depth_blocks):
    active = depth_blocks > STEP
    flags = active.astype(jnp.int32)
    ranked = jnp.cumsum(flags, axis=1) - 1
    slot_ids = jnp.arange(CAP, dtype=jnp.int32)
    matched = (ranked[:, None, :] == slot_ids[None, :, None]) & active[:, None, :]
    places = jnp.arange(TOK_DEV, dtype=jnp.int32)
    slot_rows = lax.optimization_barrier(jnp.sum(jnp.where(matched, places[None, None, :], 0), axis=2)).astype(jnp.int32)
    is_live = slot_ids[None, :] < lax.optimization_barrier(jnp.sum(flags, axis=1))[:, None]
    return (slot_rows, is_live)

def pick_table(table, slot_rows, is_live):
    blocks = table.reshape(N_SEQ, TOK_DEV, D)
    picked = jnp.take_along_axis(blocks, slot_rows[:, :, None], axis=1)
    picked = jnp.where(is_live[:, :, None], picked, jnp.zeros_like(picked))
    return picked.reshape(ACT, ATTENDER_AMOUNT, HDIM).astype(jnp.float32)

def narrow_float(values):
    return lax.optimization_barrier(values.astype(jnp.bfloat16)).astype(jnp.float32)

def one_document(iteration_arguments):
    sequence_probe_vectors, sequence_lookup_vectors, sequence_content_vectors, sequence_levels, sequence_routing_preacts, sequence_adjoint, attender_multiplier = iteration_arguments
    slot_rows, is_live = compact_index(sequence_levels.reshape(N_SEQ, TOK_DEV))
    live_flat = is_live.reshape(ACT)
    q_slots = pick_table(sequence_probe_vectors, slot_rows, is_live)
    k_slots = pick_table(sequence_lookup_vectors, slot_rows, is_live)
    v_slots = pick_table(sequence_content_vectors, slot_rows, is_live)
    weighted_similarity = 1.0 / math.sqrt(HDIM)
    row_order = jnp.arange(ACT, dtype=jnp.int32)
    lower_triangle = live_flat[None, :] & (row_order[None, :] <= row_order[:, None])
    bare_similarities = jnp.einsum('ihd,jhd->hij', q_slots, k_slots) * weighted_similarity
    multiplied_similarities = jnp.where(lower_triangle[None], attender_multiplier[:, None, None] * bare_similarities, -jnp.inf)
    row_max = lax.optimization_barrier(jnp.max(multiplied_similarities, axis=2, keepdims=True))
    shifted = jnp.exp(multiplied_similarities - row_max)
    probs = shifted / lax.optimization_barrier(jnp.sum(shifted, axis=2, keepdims=True))
    probs_low = narrow_float(probs)
    attn_head = jnp.einsum('hij,jhd->ihd', probs_low, v_slots)
    attn_wide = narrow_float(attn_head.reshape(ACT, D))
    logit_blocks = sequence_routing_preacts.reshape(N_SEQ, TOK_DEV)
    picked_logits = jnp.take_along_axis(logit_blocks, slot_rows, axis=1).reshape(ACT)
    sigmoid_gate = jax.nn.sigmoid(picked_logits)
    gate_value = jnp.where(live_flat, sigmoid_gate, 0.0)
    mixed = (gate_value[:, None] * attn_wide).astype(jnp.bfloat16)
    cot_wide = sequence_adjoint.astype(jnp.float32)
    gate_grad = jnp.where(live_flat, sigmoid_gate * (1.0 - sigmoid_gate) * lax.optimization_barrier(jnp.sum(cot_wide * attn_wide, axis=1)), 0.0)
    upstream = narrow_float(gate_value[:, None] * cot_wide).reshape(ACT, ATTENDER_AMOUNT, HDIM)
    grad_probs = jnp.einsum('ihd,jhd->hij', upstream, v_slots)
    inner_sum = lax.optimization_barrier(jnp.sum(probs * grad_probs, axis=2, keepdims=True))
    similarity_derivative = probs * (grad_probs - inner_sum)
    temp_part = lax.optimization_barrier(jnp.sum(similarity_derivative * bare_similarities, axis=(1, 2)))
    bare_derivative = narrow_float(similarity_derivative * (attender_multiplier[:, None, None] * weighted_similarity))
    query_grad = jnp.einsum('hij,jhd->ihd', bare_derivative, k_slots).astype(jnp.bfloat16).reshape(ACT, D)
    key_grad = jnp.einsum('hij,ihd->jhd', bare_derivative, q_slots).astype(jnp.bfloat16).reshape(ACT, D)
    value_grad = jnp.einsum('hij,ihd->jhd', probs_low, upstream).astype(jnp.bfloat16).reshape(ACT, D)
    return (mixed, gate_grad, query_grad, key_grad, value_grad, temp_part)

def reference(probe_vectors, lookup_vectors, content_vectors, recursion_levels, routing_preactivations, attender_multiplier, upstream_adjoint):
    attender_tiled = jnp.broadcast_to(attender_multiplier[None, :], (SEQUENCE_AMOUNT, ATTENDER_AMOUNT))
    results = lax.map(one_document, (probe_vectors, lookup_vectors, content_vectors, recursion_levels, routing_preactivations, upstream_adjoint, attender_tiled))
    mixed, gate_grad, query_grad, key_grad, value_grad, temp_parts = results
    return (mixed, gate_grad, query_grad, key_grad, value_grad, lax.optimization_barrier(jnp.sum(temp_parts, axis=0)))
```

```python
import functools
import math

import jax
import jax.numpy as jnp
from jax import lax
from jax.experimental import pallas as pl
from jax.experimental.pallas import tpu as pltpu
from jax.sharding import PartitionSpec as P

STEP = 2
MESH = pl.DeviceIdType.MESH
BF16 = jnp.bfloat16
F32 = jnp.float32


def kernel(
    n,
    reps,
    cap,
    hd,
    q_hbm,
    k_hbm,
    v_hbm,
    lev_hbm,
    logit_hbm,
    mult_ref,
    cot_hbm,
    mixed_ref,
    gg_ref,
    dq_ref,
    dk_ref,
    dv_ref,
    dm_ref,
    q_in,
    k_in,
    v_in,
    cot_in,
    lev_in,
    logit_in,
    send_a,
    send_b,
    send_c,
    recv_a,
    recv_b,
    recv_c,
    out_o,
    out_q,
    out_k,
    out_v,
    attn_in,
    dm_all,
    local_sem,
    send_sem,
    recv_sem,
    dm_send,
    dm_recv,
):
    me = lax.axis_index("seq")
    my_rep = lax.axis_index("rep")
    total = n * cap
    scale = 1.0 / math.sqrt(hd)

    def local_copy(src, dst, s):
        return pltpu.make_async_copy(src, dst, local_sem.at[s])

    lev_copy = local_copy(lev_hbm, lev_in, 0)
    logit_copy = local_copy(logit_hbm, logit_in, 1)
    q_copy = local_copy(q_hbm.at[0], q_in, 2)
    k_copy = local_copy(k_hbm.at[0], k_in, 3)
    v_copy = local_copy(v_hbm.at[0], v_in, 4)
    cot_copy = local_copy(cot_hbm.at[0], cot_in, 5)
    for c in (lev_copy, logit_copy, q_copy, k_copy, v_copy, cot_copy):
        c.start()

    def peer_loop(f):
        if n <= 8:
            for step in range(1, n):
                f(lax.rem(me + step, n))
        else:

            def body(step, carry):
                f(lax.rem(me + step, n))
                return carry

            lax.fori_loop(1, n, body, 0)

    barrier = pltpu.get_barrier_semaphore()
    peer_loop(
        lambda d: pl.semaphore_signal(
            barrier, inc=1, device_id={"seq": d}, device_id_type=MESH
        )
    )
    for r in range(1, reps):
        pl.semaphore_signal(
            barrier,
            inc=1,
            device_id={"rep": lax.rem(my_rep + r, reps)},
            device_id_type=MESH,
        )

    lev_copy.wait()
    tokens = lev_in.shape[1]
    active = lev_in[...] > STEP
    flags = jnp.where(active, 1.0, 0.0)
    upto = jnp.where(
        lax.broadcasted_iota(jnp.int32, (tokens, tokens), 0)
        <= lax.broadcasted_iota(jnp.int32, (tokens, tokens), 1),
        1.0,
        0.0,
    ).astype(BF16)
    ranked = jnp.dot(
        jnp.broadcast_to(flags, (16, tokens)).astype(BF16), upto, preferred_element_type=F32
    )[0:1] - 1.0
    slot_ids = lax.broadcasted_iota(jnp.int32, (cap, tokens), 0).astype(F32)
    matched = (ranked == slot_ids) & active
    chosen = jnp.where(matched, 1.0, 0.0)
    pick = chosen.astype(BF16)
    live = jnp.sum(chosen, axis=1, keepdims=True) > 0.5
    count = jnp.sum(flags, axis=1, keepdims=True)

    for h in range(n):
        send_a[h, 2 * cap :, :] = jnp.broadcast_to(count, (16, hd)).astype(BF16)

    def gather(src, dst, row):
        for c in range(0, n, 2):
            part = jnp.dot(
                pick, src[:, c * hd : (c + 2) * hd], preferred_element_type=F32
            ).astype(BF16)
            dst[c, row : row + cap, :] = part[:, :hd]
            dst[c + 1, row : row + cap, :] = part[:, hd:]

    def to_head(part, src, dst):
        def copy(d, slot):
            return pltpu.make_async_remote_copy(
                src_ref=src.at[d],
                dst_ref=dst.at[slot],
                send_sem=send_sem.at[part, d],
                recv_sem=recv_sem.at[part, slot],
                device_id={"seq": d},
                device_id_type=MESH,
            )

        return copy

    copy_a = to_head(0, send_a, recv_a)
    copy_b = to_head(1, send_b, recv_b)
    copy_c = to_head(2, send_c, recv_c)

    q_copy.wait()
    gather(q_in, send_a, 0)
    k_copy.wait()
    gather(k_in, send_a, cap)
    pl.semaphore_wait(barrier, n - 1 + reps - 1)
    peer_loop(lambda d: copy_a(d, me).start())
    recv_a[me] = send_a[me]

    v_copy.wait()
    gather(v_in, send_b, 0)
    peer_loop(lambda d: copy_b(d, me).start())
    recv_b[me] = send_b[me]

    logit_copy.wait()
    logits = jnp.sum(jnp.where(matched, logit_in[...], 0.0), axis=1, keepdims=True)
    sig = jax.nn.sigmoid(logits)
    gate = jnp.where(live, sig, 0.0)
    cot_copy.wait()
    for h in range(n):
        send_c[h] = (gate * cot_in[:, h * hd : (h + 1) * hd].astype(F32)).astype(BF16)
    peer_loop(lambda d: copy_c(d, me).start())
    recv_c[me] = send_c[me]

    temp = mult_ref[me]
    peer_loop(lambda d: copy_a(d, d).wait_recv())
    q_all = recv_a[:, 0:cap, :].reshape(total, hd)
    k_all = recv_a[:, cap : 2 * cap, :].reshape(total, hd)
    rows = min(total, 256)
    blocks = total // rows
    lane = lax.broadcasted_iota(jnp.int32, (1, hd), 1)
    per = hd // cap
    pieces = []
    for c in range(total // hd):
        counts = jnp.zeros((1, hd), F32)
        for b in range(per):
            got = recv_a[c * per + b, 2 * cap :, :].astype(F32)[0:1]
            counts = jnp.where(lane // cap == b, got, counts)
        pieces.append(jnp.where((lane % cap).astype(F32) < counts, 1.0, 0.0))
    live_keys = jnp.concatenate(pieces, axis=1) > 0.5

    NT = (((1,), (1,)), ((), ()))
    TN = (((0,), (0,)), ((), ()))
    plains, probs, lows = [], [], []
    for rb in range(blocks):
        end = (rb + 1) * rows
        plain = (
            lax.dot_general(
                q_all[rb * rows : end], k_all[:end], NT, preferred_element_type=F32
            )
            * scale
        )
        row_id = lax.broadcasted_iota(jnp.int32, (rows, end), 0) + rb * rows
        col_id = lax.broadcasted_iota(jnp.int32, (rows, end), 1)
        allowed = (col_id <= row_id) & live_keys[:, :end]
        scores = jnp.where(allowed, temp * plain, -jnp.inf)
        top = jnp.max(scores, axis=1, keepdims=True)
        shifted = jnp.exp(scores - top)
        prob = shifted * (1.0 / jnp.sum(shifted, axis=1, keepdims=True))
        plains.append(plain)
        probs.append(prob)
        lows.append(prob.astype(BF16))

    def to_slots(part, src, dst):
        def copy(d, slot):
            return pltpu.make_async_remote_copy(
                src_ref=src.at[pl.ds(pl.multiple_of(d * cap, cap), cap), :],
                dst_ref=dst.at[:, pl.ds(pl.multiple_of(slot * hd, hd), hd)],
                send_sem=send_sem.at[part, d],
                recv_sem=recv_sem.at[part, slot],
                device_id={"seq": d},
                device_id_type=MESH,
            )

        return copy

    copy_o = to_slots(3, out_o, attn_in)
    copy_v = to_slots(4, out_v, dv_ref.at[0])
    copy_q = to_slots(5, out_q, dq_ref.at[0])
    copy_k = to_slots(6, out_k, dk_ref.at[0])

    def finish(copy, src, dst):
        peer_loop(lambda d: copy(d, me).start())
        mine = src[pl.ds(pl.multiple_of(me * cap, cap), cap), :]
        dst[:, pl.ds(pl.multiple_of(me * hd, hd), hd)] = mine

    peer_loop(lambda d: copy_b(d, d).wait_recv())
    v_all = recv_b[...].reshape(total, hd)
    for rb in range(blocks):
        end = (rb + 1) * rows
        out_o[rb * rows : end, :] = jnp.dot(
            lows[rb], v_all[:end], preferred_element_type=F32
        ).astype(BF16)
    finish(copy_o, out_o, attn_in)

    peer_loop(lambda d: copy_c(d, d).wait_recv())
    u_all = recv_c[...].reshape(total, hd)

    def column_sums(left, right):
        tiles = [None] * blocks
        for rb in range(blocks):
            end = (rb + 1) * rows
            got = lax.dot_general(
                left[rb], right[rb * rows : end], TN, preferred_element_type=F32
            )
            for kb in range(rb + 1):
                tile = got[kb * rows : (kb + 1) * rows]
                tiles[kb] = tile if tiles[kb] is None else tiles[kb] + tile
        return tiles

    for kb, tile in enumerate(column_sums(lows, u_all)):
        out_v[kb * rows : (kb + 1) * rows, :] = tile.astype(BF16)
    finish(copy_v, out_v, dv_ref.at[0])

    lowered = []
    dm = jnp.zeros((1, 1), F32)
    for rb in range(blocks):
        end = (rb + 1) * rows
        grad_probs = lax.dot_general(
            u_all[rb * rows : end], v_all[:end], NT, preferred_element_type=F32
        )
        inner = jnp.sum(probs[rb] * grad_probs, axis=1, keepdims=True)
        grad_score = probs[rb] * (grad_probs - inner)
        by_row = jnp.sum(grad_score * plains[rb], axis=1, keepdims=True)
        dm = dm + jnp.sum(by_row, axis=0, keepdims=True)
        low = (grad_score * (temp * scale)).astype(BF16)
        lowered.append(low)
        out_q[rb * rows : end, :] = jnp.dot(
            low, k_all[:end], preferred_element_type=F32
        ).astype(BF16)
    finish(copy_q, out_q, dq_ref.at[0])
    for kb, tile in enumerate(column_sums(lowered, q_all)):
        out_k[kb * rows : (kb + 1) * rows, :] = tile.astype(BF16)
    finish(copy_k, out_k, dk_ref.at[0])

    dm_all[my_rep] = jnp.broadcast_to(dm, (8, 128))

    def copy_dm(r, slot):
        return pltpu.make_async_remote_copy(
            src_ref=dm_all.at[slot],
            dst_ref=dm_all.at[slot],
            send_sem=dm_send.at[r],
            recv_sem=dm_recv.at[slot],
            device_id={"rep": r},
            device_id_type=MESH,
        )

    for r in range(1, reps):
        copy_dm(lax.rem(my_rep + r, reps), my_rep).start()

    peer_loop(lambda d: copy_o(d, d).wait_recv())
    attn = attn_in[...].astype(F32)
    mixed_ref[0] = (gate * attn).astype(BF16)
    dots = jnp.sum(cot_in[...].astype(F32) * attn, axis=1, keepdims=True)
    grad_gate = jnp.where(live, sig * (1.0 - sig) * dots, 0.0)
    diagonal = lax.broadcasted_iota(jnp.int32, (cap, cap), 0) == lax.broadcasted_iota(
        jnp.int32, (cap, cap), 1
    )
    gg_ref[...] = jnp.sum(jnp.where(diagonal, grad_gate, 0.0), axis=0, keepdims=True)

    for r in range(1, reps):
        other = lax.rem(my_rep + r, reps)
        copy_dm(other, other).wait_recv()
    summed = dm_all[0]
    for r in range(1, reps):
        summed = summed + dm_all[r]
    dm_ref[...] = summed[0:1]

    for copy in (copy_v, copy_q, copy_k):
        peer_loop(lambda d: copy(d, d).wait_recv())
    for copy in (copy_a, copy_b, copy_c, copy_o, copy_v, copy_q, copy_k):
        peer_loop(lambda d: copy(d, me).wait_send())
    for r in range(1, reps):
        copy_dm(lax.rem(my_rep + r, reps), my_rep).wait_send()


def local(n, reps, q, k, v, levels, logits, mult, cot):
    tokens, width = q.shape[1], q.shape[2]
    cap = cot.shape[1]
    hd = width // mult.shape[0]
    total = n * cap
    anyspec = pl.BlockSpec(memory_space=pl.ANY)
    vm = pl.BlockSpec(memory_space=pltpu.VMEM)
    wide = jax.ShapeDtypeStruct((1, cap, width), BF16)
    outs = pl.pallas_call(
        functools.partial(kernel, n, reps, cap, hd),
        out_shape=(
            wide,
            jax.ShapeDtypeStruct((1, cap), F32),
            wide,
            wide,
            wide,
            jax.ShapeDtypeStruct((1, 128), F32),
        ),
        in_specs=[anyspec] * 5 + [pl.BlockSpec(memory_space=pltpu.SMEM), anyspec],
        out_specs=(vm,) * 6,
        scratch_shapes=[
            pltpu.VMEM((tokens, width), BF16),
            pltpu.VMEM((tokens, width), BF16),
            pltpu.VMEM((tokens, width), BF16),
            pltpu.VMEM((cap, width), BF16),
            pltpu.VMEM((1, tokens), jnp.int32),
            pltpu.VMEM((1, tokens), F32),
            pltpu.VMEM((n, 2 * cap + 16, hd), BF16),
            pltpu.VMEM((n, cap, hd), BF16),
            pltpu.VMEM((n, cap, hd), BF16),
            pltpu.VMEM((n, 2 * cap + 16, hd), BF16),
            pltpu.VMEM((n, cap, hd), BF16),
            pltpu.VMEM((n, cap, hd), BF16),
            pltpu.VMEM((total, hd), BF16),
            pltpu.VMEM((total, hd), BF16),
            pltpu.VMEM((total, hd), BF16),
            pltpu.VMEM((total, hd), BF16),
            pltpu.VMEM((cap, width), BF16),
            pltpu.VMEM((reps, 8, 128), F32),
            pltpu.SemaphoreType.DMA((6,)),
            pltpu.SemaphoreType.DMA((7, n)),
            pltpu.SemaphoreType.DMA((7, n)),
            pltpu.SemaphoreType.DMA((reps,)),
            pltpu.SemaphoreType.DMA((reps,)),
        ],
        compiler_params=pltpu.CompilerParams(
            collective_id=0, has_side_effects=True, vmem_limit_bytes=48 * 1024 * 1024
        ),
    )(q, k, v, levels, logits, mult, cot)
    mixed, gg, dq, dk, dv, dm = outs
    return mixed, gg, dq, dk, dv, dm[0, :1]


def solution(mesh):
    n, reps = mesh.shape["seq"], mesh.shape["rep"]
    in_specs = (
        P("rep", "seq", None),
        P("rep", "seq", None),
        P("rep", "seq", None),
        P("rep", "seq"),
        P("rep", "seq"),
        P(),
        P("rep", "seq", None),
    )
    out_specs = (
        P("rep", "seq", None),
        P("rep", "seq"),
        P("rep", "seq", None),
        P("rep", "seq", None),
        P("rep", "seq", None),
        P("seq"),
    )
    return jax.shard_map(
        functools.partial(local, n, reps),
        mesh=mesh,
        in_specs=in_specs,
        out_specs=out_specs,
        check_vma=False,
    )
```

```python
import functools
import math

import jax
import jax.numpy as jnp
from jax import lax
from jax.experimental import pallas as pl
from jax.experimental.pallas import tpu as pltpu
from jax.sharding import PartitionSpec as P

STEP = 2
MESH = pl.DeviceIdType.MESH
BF16 = jnp.bfloat16
F32 = jnp.float32


def kernel(
    n,
    reps,
    cap,
    hd,
    q_hbm,
    k_hbm,
    v_hbm,
    lev_hbm,
    logit_hbm,
    mult_hbm,
    cot_hbm,
    mixed_ref,
    gg_ref,
    dq_ref,
    dk_ref,
    dv_ref,
    dm_ref,
    q_in,
    k_in,
    v_in,
    cot_in,
    lev_in,
    logit_in,
    mult_in,
    send_a,
    send_b,
    send_c,
    recv_a,
    recv_b,
    recv_c,
    out_o,
    out_q,
    out_k,
    out_v,
    attn_in,
    dm_all,
    local_sem,
    send_sem,
    recv_sem,
    dm_send,
    dm_recv,
):
    me = lax.axis_index("seq")
    my_rep = lax.axis_index("rep")
    total = n * cap
    scale = 1.0 / math.sqrt(hd)

    def local_copy(src, dst, s):
        return pltpu.make_async_copy(src, dst, local_sem.at[s])

    lev_copy = local_copy(lev_hbm, lev_in, 0)
    logit_copy = local_copy(logit_hbm, logit_in, 1)
    q_copy = local_copy(q_hbm.at[0], q_in, 2)
    k_copy = local_copy(k_hbm.at[0], k_in, 3)
    v_copy = local_copy(v_hbm.at[0], v_in, 4)
    cot_copy = local_copy(cot_hbm.at[0], cot_in, 5)
    mult_copy = local_copy(mult_hbm, mult_in, 6)
    for c in (lev_copy, q_copy, k_copy, v_copy, logit_copy, cot_copy, mult_copy):
        c.start()

    def peer_loop(f):
        if n <= 8:
            for step in range(1, n):
                f(lax.rem(me + step, n))
        else:

            def body(step, carry):
                f(lax.rem(me + step, n))
                return carry

            lax.fori_loop(1, n, body, 0)

    barrier = pltpu.get_barrier_semaphore()
    peer_loop(
        lambda d: pl.semaphore_signal(
            barrier, inc=1, device_id={"seq": d}, device_id_type=MESH
        )
    )
    for r in range(1, reps):
        pl.semaphore_signal(
            barrier,
            inc=1,
            device_id={"rep": lax.rem(my_rep + r, reps)},
            device_id_type=MESH,
        )

    lev_copy.wait()
    tokens = lev_in.shape[1]
    active = lev_in[...] > STEP
    flags = jnp.where(active, 1.0, 0.0)
    upto = jnp.where(
        lax.broadcasted_iota(jnp.int32, (tokens, tokens), 0)
        <= lax.broadcasted_iota(jnp.int32, (tokens, tokens), 1),
        1.0,
        0.0,
    ).astype(BF16)
    ranked = jnp.dot(
        jnp.broadcast_to(flags, (16, tokens)).astype(BF16), upto, preferred_element_type=F32
    )[0:1] - 1.0
    slot_ids = lax.broadcasted_iota(jnp.int32, (cap, tokens), 0).astype(F32)
    matched = (ranked == slot_ids) & active
    chosen = jnp.where(matched, 1.0, 0.0)
    pick = chosen.astype(BF16)
    live = jnp.sum(chosen, axis=1, keepdims=True) > 0.5
    count = jnp.sum(flags, axis=1, keepdims=True)

    for h in range(n):
        send_a[h, 2 * cap :, :] = jnp.broadcast_to(count, (16, hd)).astype(BF16)

    def gather(src, dst, row):
        for c in range(0, n, 2):
            part = jnp.dot(
                pick, src[:, c * hd : (c + 2) * hd], preferred_element_type=F32
            ).astype(BF16)
            dst[c, row : row + cap, :] = part[:, :hd]
            dst[c + 1, row : row + cap, :] = part[:, hd:]

    def to_head(part, src, dst):
        def copy(d, slot):
            return pltpu.make_async_remote_copy(
                src_ref=src.at[d],
                dst_ref=dst.at[slot],
                send_sem=send_sem.at[part, d],
                recv_sem=recv_sem.at[part, slot],
                device_id={"seq": d},
                device_id_type=MESH,
            )

        return copy

    copy_a = to_head(0, send_a, recv_a)
    copy_b = to_head(1, send_b, recv_b)
    copy_c = to_head(2, send_c, recv_c)

    q_copy.wait()
    gather(q_in, send_a, 0)
    k_copy.wait()
    gather(k_in, send_a, cap)
    pl.semaphore_wait(barrier, n - 1 + reps - 1)
    peer_loop(lambda d: copy_a(d, me).start())
    recv_a[me] = send_a[me]

    v_copy.wait()
    gather(v_in, send_b, 0)
    peer_loop(lambda d: copy_b(d, me).start())
    recv_b[me] = send_b[me]

    logit_copy.wait()
    logits = jnp.sum(jnp.where(matched, logit_in[...], 0.0), axis=1, keepdims=True)
    sig = jax.nn.sigmoid(logits)
    gate = jnp.where(live, sig, 0.0)
    cot_copy.wait()
    for h in range(n):
        send_c[h] = (gate * cot_in[:, h * hd : (h + 1) * hd].astype(F32)).astype(BF16)
    peer_loop(lambda d: copy_c(d, me).start())
    recv_c[me] = send_c[me]

    mult_copy.wait()
    heads = lax.broadcasted_iota(jnp.int32, mult_in.shape, 1)
    temp = jnp.sum(jnp.where(heads == me, mult_in[...], 0.0), axis=1, keepdims=True)
    peer_loop(lambda d: copy_a(d, d).wait_recv())
    q_all = recv_a[:, 0:cap, :].reshape(total, hd)
    k_all = recv_a[:, cap : 2 * cap, :].reshape(total, hd)
    rows = min(total, 256)
    blocks = total // rows
    lane = lax.broadcasted_iota(jnp.int32, (1, hd), 1)
    per = hd // cap
    pieces = []
    for c in range(total // hd):
        counts = jnp.zeros((1, hd), F32)
        for b in range(per):
            got = recv_a[c * per + b, 2 * cap :, :].astype(F32)[0:1]
            counts = jnp.where(lane // cap == b, got, counts)
        pieces.append(jnp.where((lane % cap).astype(F32) < counts, 1.0, 0.0))
    live_keys = jnp.concatenate(pieces, axis=1) > 0.5

    NT = (((1,), (1,)), ((), ()))
    TN = (((0,), (0,)), ((), ()))
    plains, probs, lows = [], [], []
    for rb in range(blocks):
        end = (rb + 1) * rows
        plain = (
            lax.dot_general(
                q_all[rb * rows : end], k_all[:end], NT, preferred_element_type=F32
            )
            * scale
        )
        row_id = lax.broadcasted_iota(jnp.int32, (rows, end), 0) + rb * rows
        col_id = lax.broadcasted_iota(jnp.int32, (rows, end), 1)
        allowed = (col_id <= row_id) & live_keys[:, :end]
        scores = jnp.where(allowed, temp * plain, -jnp.inf)
        top = jnp.max(scores, axis=1, keepdims=True)
        shifted = jnp.exp(scores - top)
        prob = shifted * (1.0 / jnp.sum(shifted, axis=1, keepdims=True))
        plains.append(plain)
        probs.append(prob)
        lows.append(prob.astype(BF16))

    def to_slots(part, src, dst):
        def copy(d, slot):
            return pltpu.make_async_remote_copy(
                src_ref=src.at[pl.ds(pl.multiple_of(d * cap, cap), cap), :],
                dst_ref=dst.at[:, pl.ds(pl.multiple_of(slot * hd, hd), hd)],
                send_sem=send_sem.at[part, d],
                recv_sem=recv_sem.at[part, slot],
                device_id={"seq": d},
                device_id_type=MESH,
            )

        return copy

    copy_o = to_slots(3, out_o, attn_in)
    copy_v = to_slots(4, out_v, dv_ref.at[0])
    copy_q = to_slots(5, out_q, dq_ref.at[0])
    copy_k = to_slots(6, out_k, dk_ref.at[0])

    def finish(copy, src, dst):
        peer_loop(lambda d: copy(d, me).start())
        mine = src[pl.ds(pl.multiple_of(me * cap, cap), cap), :]
        dst[:, pl.ds(pl.multiple_of(me * hd, hd), hd)] = mine

    peer_loop(lambda d: copy_b(d, d).wait_recv())
    v_all = recv_b[...].reshape(total, hd)
    for rb in range(blocks):
        end = (rb + 1) * rows
        out_o[rb * rows : end, :] = jnp.dot(
            lows[rb], v_all[:end], preferred_element_type=F32
        ).astype(BF16)
    finish(copy_o, out_o, attn_in)

    peer_loop(lambda d: copy_c(d, d).wait_recv())
    u_all = recv_c[...].reshape(total, hd)

    def column_sums(left, right):
        tiles = [None] * blocks
        for rb in range(blocks):
            end = (rb + 1) * rows
            got = lax.dot_general(
                left[rb], right[rb * rows : end], TN, preferred_element_type=F32
            )
            for kb in range(rb + 1):
                tile = got[kb * rows : (kb + 1) * rows]
                tiles[kb] = tile if tiles[kb] is None else tiles[kb] + tile
        return tiles

    for kb, tile in enumerate(column_sums(lows, u_all)):
        out_v[kb * rows : (kb + 1) * rows, :] = tile.astype(BF16)
    finish(copy_v, out_v, dv_ref.at[0])

    lowered = []
    dm = jnp.zeros((1, 1), F32)
    for rb in range(blocks):
        end = (rb + 1) * rows
        grad_probs = lax.dot_general(
            u_all[rb * rows : end], v_all[:end], NT, preferred_element_type=F32
        )
        inner = jnp.sum(probs[rb] * grad_probs, axis=1, keepdims=True)
        grad_score = probs[rb] * (grad_probs - inner)
        by_row = jnp.sum(grad_score * plains[rb], axis=1, keepdims=True)
        dm = dm + jnp.sum(by_row, axis=0, keepdims=True)
        low = (grad_score * (temp * scale)).astype(BF16)
        lowered.append(low)
        out_q[rb * rows : end, :] = jnp.dot(
            low, k_all[:end], preferred_element_type=F32
        ).astype(BF16)
    finish(copy_q, out_q, dq_ref.at[0])
    for kb, tile in enumerate(column_sums(lowered, q_all)):
        out_k[kb * rows : (kb + 1) * rows, :] = tile.astype(BF16)
    finish(copy_k, out_k, dk_ref.at[0])

    dm_all[my_rep] = jnp.broadcast_to(dm, (8, 128))

    def copy_dm(r, slot):
        return pltpu.make_async_remote_copy(
            src_ref=dm_all.at[slot],
            dst_ref=dm_all.at[slot],
            send_sem=dm_send.at[r],
            recv_sem=dm_recv.at[slot],
            device_id={"rep": r},
            device_id_type=MESH,
        )

    for r in range(1, reps):
        copy_dm(lax.rem(my_rep + r, reps), my_rep).start()

    peer_loop(lambda d: copy_o(d, d).wait_recv())
    attn = attn_in[...].astype(F32)
    mixed_ref[0] = (gate * attn).astype(BF16)
    dots = jnp.sum(cot_in[...].astype(F32) * attn, axis=1, keepdims=True)
    grad_gate = jnp.where(live, sig * (1.0 - sig) * dots, 0.0)
    diagonal = lax.broadcasted_iota(jnp.int32, (cap, cap), 0) == lax.broadcasted_iota(
        jnp.int32, (cap, cap), 1
    )
    gg_ref[...] = jnp.sum(jnp.where(diagonal, grad_gate, 0.0), axis=0, keepdims=True)

    for r in range(1, reps):
        other = lax.rem(my_rep + r, reps)
        copy_dm(other, other).wait_recv()
    summed = dm_all[0]
    for r in range(1, reps):
        summed = summed + dm_all[r]
    dm_ref[...] = summed[0:1, 0:1]

    for copy in (copy_v, copy_q, copy_k):
        peer_loop(lambda d: copy(d, d).wait_recv())
    for copy in (copy_a, copy_b, copy_c, copy_o, copy_v, copy_q, copy_k):
        peer_loop(lambda d: copy(d, me).wait_send())
    for r in range(1, reps):
        copy_dm(lax.rem(my_rep + r, reps), my_rep).wait_send()


def store(*refs):
    ins, outs, held, got, put = refs[:6], refs[6:12], refs[12:18], refs[18], refs[19]
    reads = [pltpu.make_async_copy(ins[i], held[i], got.at[i]) for i in range(6)]
    writes = [pltpu.make_async_copy(held[i], outs[i], put.at[i]) for i in range(6)]
    for c in reads:
        c.start()
    for r, w in zip(reads, writes):
        r.wait()
        w.start()
    for c in writes:
        c.wait()


def local(n, reps, q, k, v, levels, logits, mult, cot):
    tokens, width = q.shape[1], q.shape[2]
    cap = cot.shape[1]
    hd = width // mult.shape[0]
    total = n * cap
    far = pl.BlockSpec(memory_space=pltpu.HBM)
    vm = pl.BlockSpec(memory_space=pltpu.VMEM)
    wide = jax.ShapeDtypeStruct((1, cap, width), BF16)
    outs = pl.pallas_call(
        functools.partial(kernel, n, reps, cap, hd),
        out_shape=(
            wide,
            jax.ShapeDtypeStruct((1, cap), F32),
            wide,
            wide,
            wide,
            jax.ShapeDtypeStruct((1, 1), F32),
        ),
        in_specs=[far] * 7,
        out_specs=(vm,) * 6,
        scratch_shapes=[
            pltpu.VMEM((tokens, width), BF16),
            pltpu.VMEM((tokens, width), BF16),
            pltpu.VMEM((tokens, width), BF16),
            pltpu.VMEM((cap, width), BF16),
            pltpu.VMEM((1, tokens), jnp.int32),
            pltpu.VMEM((1, tokens), F32),
            pltpu.VMEM((1, n), F32),
            pltpu.VMEM((n, 2 * cap + 16, hd), BF16),
            pltpu.VMEM((n, cap, hd), BF16),
            pltpu.VMEM((n, cap, hd), BF16),
            pltpu.VMEM((n, 2 * cap + 16, hd), BF16),
            pltpu.VMEM((n, cap, hd), BF16),
            pltpu.VMEM((n, cap, hd), BF16),
            pltpu.VMEM((total, hd), BF16),
            pltpu.VMEM((total, hd), BF16),
            pltpu.VMEM((total, hd), BF16),
            pltpu.VMEM((total, hd), BF16),
            pltpu.VMEM((cap, width), BF16),
            pltpu.VMEM((reps, 8, 128), F32),
            pltpu.SemaphoreType.DMA((7,)),
            pltpu.SemaphoreType.DMA((7, n)),
            pltpu.SemaphoreType.DMA((7, n)),
            pltpu.SemaphoreType.DMA((reps,)),
            pltpu.SemaphoreType.DMA((reps,)),
        ],
        compiler_params=pltpu.CompilerParams(
            collective_id=0, has_side_effects=True, vmem_limit_bytes=56 * 1024 * 1024
        ),
    )(q, k, v, levels, logits, mult.reshape(1, n), cot)
    mixed, gg, dq, dk, dv, dm = pl.pallas_call(
        store,
        out_shape=tuple(jax.ShapeDtypeStruct(o.shape, o.dtype) for o in outs),
        in_specs=[far] * 6,
        out_specs=(far,) * 6,
        scratch_shapes=[pltpu.VMEM(o.shape, o.dtype) for o in outs]
        + [pltpu.SemaphoreType.DMA((6,)), pltpu.SemaphoreType.DMA((6,))],
        compiler_params=pltpu.CompilerParams(vmem_limit_bytes=56 * 1024 * 1024),
    )(*outs)
    return mixed, gg, dq, dk, dv, dm[0]


def solution(mesh):
    n, reps = mesh.shape["seq"], mesh.shape["rep"]
    in_specs = (
        P("rep", "seq", None),
        P("rep", "seq", None),
        P("rep", "seq", None),
        P("rep", "seq"),
        P("rep", "seq"),
        P(),
        P("rep", "seq", None),
    )
    out_specs = (
        P("rep", "seq", None),
        P("rep", "seq"),
        P("rep", "seq", None),
        P("rep", "seq", None),
        P("rep", "seq", None),
        P("seq"),
    )
    return jax.shard_map(
        functools.partial(local, n, reps),
        mesh=mesh,
        in_specs=in_specs,
        out_specs=out_specs,
        check_vma=False,
    )
```

```python
import functools
import math

import jax
import jax.numpy as jnp
from jax import lax
from jax.experimental import pallas as pl
from jax.experimental.pallas import tpu as pltpu
from jax.sharding import PartitionSpec as P

STEP = 2
MESH = pl.DeviceIdType.MESH
BF16 = jnp.bfloat16
F32 = jnp.float32


def kernel(
    n,
    reps,
    cap,
    hd,
    q_hbm,
    k_hbm,
    v_hbm,
    lev_hbm,
    logit_hbm,
    mult_hbm,
    cot_hbm,
    mixed_hbm,
    gg_hbm,
    dq_hbm,
    dk_hbm,
    dv_hbm,
    dm_hbm,
    mixed_ref,
    gg_ref,
    dq_ref,
    dk_ref,
    dv_ref,
    dm_ref,
    q_in,
    k_in,
    v_in,
    cot_in,
    lev_in,
    logit_in,
    mult_in,
    send_a,
    send_b,
    send_c,
    recv_a,
    recv_b,
    recv_c,
    out_o,
    out_q,
    out_k,
    out_v,
    attn_in,
    dm_all,
    local_sem,
    send_sem,
    recv_sem,
    dm_send,
    dm_recv,
):
    me = lax.axis_index("seq")
    my_rep = lax.axis_index("rep")
    total = n * cap
    scale = 1.0 / math.sqrt(hd)

    def local_copy(src, dst, s):
        return pltpu.make_async_copy(src, dst, local_sem.at[s])

    lev_copy = local_copy(lev_hbm, lev_in, 0)
    logit_copy = local_copy(logit_hbm, logit_in, 1)
    q_copy = local_copy(q_hbm.at[0], q_in, 2)
    k_copy = local_copy(k_hbm.at[0], k_in, 3)
    v_copy = local_copy(v_hbm.at[0], v_in, 4)
    cot_copy = local_copy(cot_hbm.at[0], cot_in, 5)
    mult_copy = local_copy(mult_hbm, mult_in, 6)
    for c in (lev_copy, q_copy, k_copy, v_copy, logit_copy, cot_copy, mult_copy):
        c.start()

    def peer_loop(f):
        if n <= 8:
            for step in range(1, n):
                f(lax.rem(me + step, n))
        else:

            def body(step, carry):
                f(lax.rem(me + step, n))
                return carry

            lax.fori_loop(1, n, body, 0)

    barrier = pltpu.get_barrier_semaphore()
    peer_loop(
        lambda d: pl.semaphore_signal(
            barrier, inc=1, device_id={"seq": d}, device_id_type=MESH
        )
    )
    for r in range(1, reps):
        pl.semaphore_signal(
            barrier,
            inc=1,
            device_id={"rep": lax.rem(my_rep + r, reps)},
            device_id_type=MESH,
        )

    lev_copy.wait()
    tokens = lev_in.shape[1]
    active = lev_in[...] > STEP
    flags = jnp.where(active, 1.0, 0.0)
    upto = jnp.where(
        lax.broadcasted_iota(jnp.int32, (tokens, tokens), 0)
        <= lax.broadcasted_iota(jnp.int32, (tokens, tokens), 1),
        1.0,
        0.0,
    ).astype(BF16)
    ranked = jnp.dot(
        jnp.broadcast_to(flags, (16, tokens)).astype(BF16), upto, preferred_element_type=F32
    )[0:1] - 1.0
    slot_ids = lax.broadcasted_iota(jnp.int32, (cap, tokens), 0).astype(F32)
    matched = (ranked == slot_ids) & active
    chosen = jnp.where(matched, 1.0, 0.0)
    pick = chosen.astype(BF16)
    live = jnp.sum(chosen, axis=1, keepdims=True) > 0.5
    count = jnp.sum(flags, axis=1, keepdims=True)

    for h in range(n):
        send_a[h, 2 * cap :, :] = jnp.broadcast_to(count, (16, hd)).astype(BF16)

    def gather(src, dst, row):
        for c in range(0, n, 2):
            part = jnp.dot(
                pick, src[:, c * hd : (c + 2) * hd], preferred_element_type=F32
            ).astype(BF16)
            dst[c, row : row + cap, :] = part[:, :hd]
            dst[c + 1, row : row + cap, :] = part[:, hd:]

    def to_head(part, src, dst):
        def copy(d, slot):
            return pltpu.make_async_remote_copy(
                src_ref=src.at[d],
                dst_ref=dst.at[slot],
                send_sem=send_sem.at[part, d],
                recv_sem=recv_sem.at[part, slot],
                device_id={"seq": d},
                device_id_type=MESH,
            )

        return copy

    copy_a = to_head(0, send_a, recv_a)
    copy_b = to_head(1, send_b, recv_b)
    copy_c = to_head(2, send_c, recv_c)

    q_copy.wait()
    gather(q_in, send_a, 0)
    k_copy.wait()
    gather(k_in, send_a, cap)
    pl.semaphore_wait(barrier, n - 1 + reps - 1)
    peer_loop(lambda d: copy_a(d, me).start())
    recv_a[me] = send_a[me]

    v_copy.wait()
    gather(v_in, send_b, 0)
    peer_loop(lambda d: copy_b(d, me).start())
    recv_b[me] = send_b[me]

    logit_copy.wait()
    logits = jnp.sum(jnp.where(matched, logit_in[...], 0.0), axis=1, keepdims=True)
    sig = jax.nn.sigmoid(logits)
    gate = jnp.where(live, sig, 0.0)
    cot_copy.wait()
    for h in range(n):
        send_c[h] = (gate * cot_in[:, h * hd : (h + 1) * hd].astype(F32)).astype(BF16)
    peer_loop(lambda d: copy_c(d, me).start())
    recv_c[me] = send_c[me]

    mult_copy.wait()
    heads = lax.broadcasted_iota(jnp.int32, mult_in.shape, 1)
    temp = jnp.sum(jnp.where(heads == me, mult_in[...], 0.0), axis=1, keepdims=True)
    peer_loop(lambda d: copy_a(d, d).wait_recv())
    q_all = recv_a[:, 0:cap, :].reshape(total, hd)
    k_all = recv_a[:, cap : 2 * cap, :].reshape(total, hd)
    rows = min(total, 128)
    blocks = total // rows
    lane = lax.broadcasted_iota(jnp.int32, (1, hd), 1)
    per = hd // cap
    pieces = []
    for c in range(total // hd):
        counts = jnp.zeros((1, hd), F32)
        for b in range(per):
            got = recv_a[c * per + b, 2 * cap :, :].astype(F32)[0:1]
            counts = jnp.where(lane // cap == b, got, counts)
        pieces.append(jnp.where((lane % cap).astype(F32) < counts, 1.0, 0.0))
    live_keys = jnp.concatenate(pieces, axis=1) > 0.5

    NT = (((1,), (1,)), ((), ()))
    TN = (((0,), (0,)), ((), ()))
    plains, probs, lows = [], [], []
    for rb in range(blocks):
        end = (rb + 1) * rows
        plain = (
            lax.dot_general(
                q_all[rb * rows : end], k_all[:end], NT, preferred_element_type=F32
            )
            * scale
        )
        row_id = lax.broadcasted_iota(jnp.int32, (rows, end), 0) + rb * rows
        col_id = lax.broadcasted_iota(jnp.int32, (rows, end), 1)
        allowed = (col_id <= row_id) & live_keys[:, :end]
        scores = jnp.where(allowed, temp * plain, -jnp.inf)
        top = jnp.max(scores, axis=1, keepdims=True)
        shifted = jnp.exp(scores - top)
        prob = shifted * (1.0 / jnp.sum(shifted, axis=1, keepdims=True))
        plains.append(plain)
        probs.append(prob)
        lows.append(prob.astype(BF16))

    def to_slots(part, src, dst):
        def copy(d, slot):
            return pltpu.make_async_remote_copy(
                src_ref=src.at[pl.ds(pl.multiple_of(d * cap, cap), cap), :],
                dst_ref=dst.at[:, pl.ds(pl.multiple_of(slot * hd, hd), hd)],
                send_sem=send_sem.at[part, d],
                recv_sem=recv_sem.at[part, slot],
                device_id={"seq": d},
                device_id_type=MESH,
            )

        return copy

    copy_o = to_slots(3, out_o, attn_in)
    copy_v = to_slots(4, out_v, dv_hbm.at[0])
    copy_q = to_slots(5, out_q, dq_hbm.at[0])
    copy_k = to_slots(6, out_k, dk_hbm.at[0])

    def finish(copy, src, dst, sem):
        peer_loop(lambda d: copy(d, me).start())
        return pltpu.make_async_copy(
            src.at[pl.ds(pl.multiple_of(me * cap, cap), cap), :],
            dst.at[:, pl.ds(pl.multiple_of(me * hd, hd), hd)],
            local_sem.at[sem],
        )

    peer_loop(lambda d: copy_b(d, d).wait_recv())
    v_all = recv_b[...].reshape(total, hd)
    for rb in range(blocks):
        end = (rb + 1) * rows
        out_o[rb * rows : end, :] = jnp.dot(
            lows[rb], v_all[:end], preferred_element_type=F32
        ).astype(BF16)
    own_o = finish(copy_o, out_o, attn_in, 13)
    own_o.start()

    peer_loop(lambda d: copy_c(d, d).wait_recv())
    u_all = recv_c[...].reshape(total, hd)

    def column_sums(left, right):
        tiles = [None] * blocks
        for rb in range(blocks):
            end = (rb + 1) * rows
            got = lax.dot_general(
                left[rb], right[rb * rows : end], TN, preferred_element_type=F32
            )
            for kb in range(rb + 1):
                tile = got[kb * rows : (kb + 1) * rows]
                tiles[kb] = tile if tiles[kb] is None else tiles[kb] + tile
        return tiles

    for kb, tile in enumerate(column_sums(lows, u_all)):
        out_v[kb * rows : (kb + 1) * rows, :] = tile.astype(BF16)
    own_v = finish(copy_v, out_v, dv_hbm.at[0], 12)
    own_v.start()

    lowered = []
    dm = jnp.zeros((1, 1), F32)
    for rb in range(blocks):
        end = (rb + 1) * rows
        grad_probs = lax.dot_general(
            u_all[rb * rows : end], v_all[:end], NT, preferred_element_type=F32
        )
        inner = jnp.sum(probs[rb] * grad_probs, axis=1, keepdims=True)
        grad_score = probs[rb] * (grad_probs - inner)
        by_row = jnp.sum(grad_score * plains[rb], axis=1, keepdims=True)
        dm = dm + jnp.sum(by_row, axis=0, keepdims=True)
        low = (grad_score * (temp * scale)).astype(BF16)
        lowered.append(low)
        out_q[rb * rows : end, :] = jnp.dot(
            low, k_all[:end], preferred_element_type=F32
        ).astype(BF16)
    own_q = finish(copy_q, out_q, dq_hbm.at[0], 10)
    own_q.start()
    for kb, tile in enumerate(column_sums(lowered, q_all)):
        out_k[kb * rows : (kb + 1) * rows, :] = tile.astype(BF16)
    own_k = finish(copy_k, out_k, dk_hbm.at[0], 11)
    own_k.start()

    dm_all[my_rep] = jnp.broadcast_to(dm, (8, 128))

    def copy_dm(r, slot):
        return pltpu.make_async_remote_copy(
            src_ref=dm_all.at[slot],
            dst_ref=dm_all.at[slot],
            send_sem=dm_send.at[r],
            recv_sem=dm_recv.at[slot],
            device_id={"rep": r},
            device_id_type=MESH,
        )

    for r in range(1, reps):
        copy_dm(lax.rem(my_rep + r, reps), my_rep).start()

    stores = [
        local_copy(a, b, 7 + i)
        for i, (a, b) in enumerate(
            (
                (mixed_ref, mixed_hbm),
                (gg_ref, gg_hbm),
                (dm_ref, dm_hbm),
            )
        )
    ]
    own_o.wait()
    peer_loop(lambda d: copy_o(d, d).wait_recv())
    attn = attn_in[...].astype(F32)
    mixed_ref[0] = (gate * attn).astype(BF16)
    dots = jnp.sum(cot_in[...].astype(F32) * attn, axis=1, keepdims=True)
    grad_gate = jnp.where(live, sig * (1.0 - sig) * dots, 0.0)
    diagonal = lax.broadcasted_iota(jnp.int32, (cap, cap), 0) == lax.broadcasted_iota(
        jnp.int32, (cap, cap), 1
    )
    gg_ref[...] = jnp.sum(jnp.where(diagonal, grad_gate, 0.0), axis=0, keepdims=True)
    stores[0].start()
    stores[1].start()

    for copy in (copy_v, copy_q):
        peer_loop(lambda d: copy(d, d).wait_recv())
    for r in range(1, reps):
        other = lax.rem(my_rep + r, reps)
        copy_dm(other, other).wait_recv()
    summed = dm_all[0]
    for r in range(1, reps):
        summed = summed + dm_all[r]
    dm_ref[...] = summed[0:1, 0:1]

    stores[2].start()
    peer_loop(lambda d: copy_k(d, d).wait_recv())
    for copy in (copy_a, copy_b, copy_c, copy_o, copy_v, copy_q, copy_k):
        peer_loop(lambda d: copy(d, me).wait_send())
    for r in range(1, reps):
        copy_dm(lax.rem(my_rep + r, reps), my_rep).wait_send()
    for c in stores + [own_v, own_q, own_k]:
        c.wait()


def store(*refs):
    ins, outs, held, got, put = refs[:6], refs[6:12], refs[12:18], refs[18], refs[19]
    reads = [pltpu.make_async_copy(ins[i], held[i], got.at[i]) for i in range(6)]
    writes = [pltpu.make_async_copy(held[i], outs[i], put.at[i]) for i in range(6)]
    for c in reads:
        c.start()
    for r, w in zip(reads, writes):
        r.wait()
        w.start()
    for c in writes:
        c.wait()


def local(n, reps, q, k, v, levels, logits, mult, cot):
    tokens, width = q.shape[1], q.shape[2]
    cap = cot.shape[1]
    hd = width // mult.shape[0]
    total = n * cap
    far = pl.BlockSpec(memory_space=pltpu.HBM)
    wide = jax.ShapeDtypeStruct((1, cap, width), BF16)
    outs = pl.pallas_call(
        functools.partial(kernel, n, reps, cap, hd),
        out_shape=(
            wide,
            jax.ShapeDtypeStruct((1, cap), F32),
            wide,
            wide,
            wide,
            jax.ShapeDtypeStruct((1, 1), F32),
        ),
        in_specs=[far] * 7,
        out_specs=(far,) * 6,
        scratch_shapes=[
            pltpu.VMEM((1, cap, width), BF16),
            pltpu.VMEM((1, cap), F32),
            pltpu.VMEM((1, cap, width), BF16),
            pltpu.VMEM((1, cap, width), BF16),
            pltpu.VMEM((1, cap, width), BF16),
            pltpu.VMEM((1, 1), F32),
            pltpu.VMEM((tokens, width), BF16),
            pltpu.VMEM((tokens, width), BF16),
            pltpu.VMEM((tokens, width), BF16),
            pltpu.VMEM((cap, width), BF16),
            pltpu.VMEM((1, tokens), jnp.int32),
            pltpu.VMEM((1, tokens), F32),
            pltpu.VMEM((1, n), F32),
            pltpu.VMEM((n, 2 * cap + 16, hd), BF16),
            pltpu.VMEM((n, cap, hd), BF16),
            pltpu.VMEM((n, cap, hd), BF16),
            pltpu.VMEM((n, 2 * cap + 16, hd), BF16),
            pltpu.VMEM((n, cap, hd), BF16),
            pltpu.VMEM((n, cap, hd), BF16),
            pltpu.VMEM((total, hd), BF16),
            pltpu.VMEM((total, hd), BF16),
            pltpu.VMEM((total, hd), BF16),
            pltpu.VMEM((total, hd), BF16),
            pltpu.VMEM((cap, width), BF16),
            pltpu.VMEM((reps, 8, 128), F32),
            pltpu.SemaphoreType.DMA((14,)),
            pltpu.SemaphoreType.DMA((7, n)),
            pltpu.SemaphoreType.DMA((7, n)),
            pltpu.SemaphoreType.DMA((reps,)),
            pltpu.SemaphoreType.DMA((reps,)),
        ],
        compiler_params=pltpu.CompilerParams(
            collective_id=0, has_side_effects=True, vmem_limit_bytes=56 * 1024 * 1024
        ),
    )(q, k, v, levels, logits, mult.reshape(1, n), cot)
    mixed, gg, dq, dk, dv, dm = pl.pallas_call(
        store,
        out_shape=tuple(jax.ShapeDtypeStruct(o.shape, o.dtype) for o in outs),
        in_specs=[far] * 6,
        out_specs=(far,) * 6,
        scratch_shapes=[pltpu.VMEM(o.shape, o.dtype) for o in outs]
        + [pltpu.SemaphoreType.DMA((6,)), pltpu.SemaphoreType.DMA((6,))],
        compiler_params=pltpu.CompilerParams(vmem_limit_bytes=56 * 1024 * 1024),
    )(*outs)
    return mixed, gg, dq, dk, dv, dm[0]


def solution(mesh):
    n, reps = mesh.shape["seq"], mesh.shape["rep"]
    in_specs = (
        P("rep", "seq", None),
        P("rep", "seq", None),
        P("rep", "seq", None),
        P("rep", "seq"),
        P("rep", "seq"),
        P(),
        P("rep", "seq", None),
    )
    out_specs = (
        P("rep", "seq", None),
        P("rep", "seq"),
        P("rep", "seq", None),
        P("rep", "seq", None),
        P("rep", "seq", None),
        P("seq"),
    )
    return jax.shard_map(
        functools.partial(local, n, reps),
        mesh=mesh,
        in_specs=in_specs,
        out_specs=out_specs,
        check_vma=False,
    )
```

```python
import functools
import math

import jax
import jax.numpy as jnp
from jax import lax
from jax.experimental import pallas as pl
from jax.experimental.pallas import tpu as pltpu
from jax.sharding import PartitionSpec as P

STEP = 2
MESH = pl.DeviceIdType.MESH
BF16 = jnp.bfloat16
F32 = jnp.float32


def kernel(
    n,
    reps,
    cap,
    hd,
    q_hbm,
    k_hbm,
    v_hbm,
    lev_hbm,
    logit_hbm,
    mult_hbm,
    cot_hbm,
    mixed_hbm,
    gg_hbm,
    dq_hbm,
    dk_hbm,
    dv_hbm,
    dm_hbm,
    mixed_ref,
    gg_ref,
    dq_ref,
    dk_ref,
    dv_ref,
    dm_ref,
    q_in,
    k_in,
    v_in,
    cot_in,
    lev_in,
    logit_in,
    mult_in,
    send_a,
    send_b,
    send_c,
    recv_a,
    recv_b,
    recv_c,
    out_o,
    out_q,
    out_k,
    out_v,
    attn_in,
    dm_all,
    local_sem,
    send_sem,
    recv_sem,
    dm_send,
    dm_recv,
):
    me = lax.axis_index("seq")
    my_rep = lax.axis_index("rep")
    total = n * cap
    scale = 1.0 / math.sqrt(hd)

    def local_copy(src, dst, s):
        return pltpu.make_async_copy(src, dst, local_sem.at[s])

    lev_copy = local_copy(lev_hbm, lev_in, 0)
    logit_copy = local_copy(logit_hbm, logit_in, 1)
    q_copy = local_copy(q_hbm.at[0], q_in, 2)
    k_copy = local_copy(k_hbm.at[0], k_in, 3)
    v_copy = local_copy(v_hbm.at[0], v_in, 4)
    cot_copy = local_copy(cot_hbm.at[0], cot_in, 5)
    mult_copy = local_copy(mult_hbm, mult_in, 6)
    for c in (lev_copy, q_copy, k_copy, v_copy, logit_copy, cot_copy, mult_copy):
        c.start()

    def peer_loop(f):
        if n <= 8:
            for step in range(1, n):
                f(lax.rem(me + step, n))
        else:

            def body(step, carry):
                f(lax.rem(me + step, n))
                return carry

            lax.fori_loop(1, n, body, 0)

    barrier = pltpu.get_barrier_semaphore()
    peer_loop(
        lambda d: pl.semaphore_signal(
            barrier, inc=1, device_id={"seq": d}, device_id_type=MESH
        )
    )
    for r in range(1, reps):
        pl.semaphore_signal(
            barrier,
            inc=1,
            device_id={"rep": lax.rem(my_rep + r, reps)},
            device_id_type=MESH,
        )

    lev_copy.wait()
    tokens = lev_in.shape[1]
    active = lev_in[...] > STEP
    flags = jnp.where(active, 1.0, 0.0)
    upto = jnp.where(
        lax.broadcasted_iota(jnp.int32, (tokens, tokens), 0)
        <= lax.broadcasted_iota(jnp.int32, (tokens, tokens), 1),
        1.0,
        0.0,
    ).astype(BF16)
    ranked = jnp.dot(
        jnp.broadcast_to(flags, (16, tokens)).astype(BF16), upto, preferred_element_type=F32
    )[0:1] - 1.0
    slot_ids = lax.broadcasted_iota(jnp.int32, (cap, tokens), 0).astype(F32)
    matched = (ranked == slot_ids) & active
    chosen = jnp.where(matched, 1.0, 0.0)
    pick = chosen.astype(BF16)
    live = jnp.sum(chosen, axis=1, keepdims=True) > 0.5
    count = jnp.sum(flags, axis=1, keepdims=True)

    for h in range(n):
        send_a[h, 2 * cap :, :] = jnp.broadcast_to(count, (16, hd)).astype(BF16)

    def gather(src, dst, row):
        for c in range(0, n, 2):
            part = jnp.dot(
                pick, src[:, c * hd : (c + 2) * hd], preferred_element_type=F32
            ).astype(BF16)
            dst[c, row : row + cap, :] = part[:, :hd]
            dst[c + 1, row : row + cap, :] = part[:, hd:]

    def to_head(part, src, dst):
        def copy(d, slot):
            return pltpu.make_async_remote_copy(
                src_ref=src.at[d],
                dst_ref=dst.at[slot],
                send_sem=send_sem.at[part, d],
                recv_sem=recv_sem.at[part, slot],
                device_id={"seq": d},
                device_id_type=MESH,
            )

        return copy

    copy_a = to_head(0, send_a, recv_a)
    copy_b = to_head(1, send_b, recv_b)
    copy_c = to_head(2, send_c, recv_c)

    q_copy.wait()
    gather(q_in, send_a, 0)
    k_copy.wait()
    gather(k_in, send_a, cap)
    pl.semaphore_wait(barrier, n - 1 + reps - 1)
    peer_loop(lambda d: copy_a(d, me).start())
    recv_a[me] = send_a[me]

    v_copy.wait()
    gather(v_in, send_b, 0)
    peer_loop(lambda d: copy_b(d, me).start())
    recv_b[me] = send_b[me]

    logit_copy.wait()
    logits = jnp.sum(jnp.where(matched, logit_in[...], 0.0), axis=1, keepdims=True)
    sig = jax.nn.sigmoid(logits)
    gate = jnp.where(live, sig, 0.0)
    cot_copy.wait()
    for h in range(n):
        send_c[h] = (gate * cot_in[:, h * hd : (h + 1) * hd].astype(F32)).astype(BF16)
    peer_loop(lambda d: copy_c(d, me).start())
    recv_c[me] = send_c[me]

    mult_copy.wait()
    heads = lax.broadcasted_iota(jnp.int32, mult_in.shape, 1)
    temp = jnp.sum(jnp.where(heads == me, mult_in[...], 0.0), axis=1, keepdims=True)
    peer_loop(lambda d: copy_a(d, d).wait_recv())
    q_all = recv_a[:, 0:cap, :].reshape(total, hd)
    k_all = recv_a[:, cap : 2 * cap, :].reshape(total, hd)
    rows = min(total, 128)
    blocks = total // rows
    lane = lax.broadcasted_iota(jnp.int32, (1, hd), 1)
    per = hd // cap
    pieces = []
    for c in range(total // hd):
        counts = jnp.zeros((1, hd), F32)
        for b in range(per):
            got = recv_a[c * per + b, 2 * cap :, :].astype(F32)[0:1]
            counts = jnp.where(lane // cap == b, got, counts)
        pieces.append(jnp.where((lane % cap).astype(F32) < counts, 1.0, 0.0))
    live_keys = jnp.concatenate(pieces, axis=1) > 0.5

    NT = (((1,), (1,)), ((), ()))
    TN = (((0,), (0,)), ((), ()))
    plains, probs, lows = [], [], []
    for rb in range(blocks):
        end = (rb + 1) * rows
        plain = (
            lax.dot_general(
                q_all[rb * rows : end], k_all[:end], NT, preferred_element_type=F32
            )
            * scale
        )
        row_id = lax.broadcasted_iota(jnp.int32, (rows, end), 0) + rb * rows
        col_id = lax.broadcasted_iota(jnp.int32, (rows, end), 1)
        allowed = (col_id <= row_id) & live_keys[:, :end]
        scores = jnp.where(allowed, temp * plain, -jnp.inf)
        top = jnp.max(scores, axis=1, keepdims=True)
        shifted = jnp.exp(scores - top)
        prob = shifted * (1.0 / jnp.sum(shifted, axis=1, keepdims=True))
        plains.append(plain)
        probs.append(prob)
        lows.append(prob.astype(BF16))

    def to_slots(part, src, dst):
        def copy(d, slot):
            return pltpu.make_async_remote_copy(
                src_ref=src.at[pl.ds(pl.multiple_of(d * cap, cap), cap), :],
                dst_ref=dst.at[:, pl.ds(pl.multiple_of(slot * hd, hd), hd)],
                send_sem=send_sem.at[part, d],
                recv_sem=recv_sem.at[part, slot],
                device_id={"seq": d},
                device_id_type=MESH,
            )

        return copy

    copy_o = to_slots(3, out_o, attn_in)
    copy_v = to_slots(4, out_v, dv_hbm.at[0])
    copy_q = to_slots(5, out_q, dq_hbm.at[0])
    copy_k = to_slots(6, out_k, dk_hbm.at[0])

    def finish(copy, src, dst, sem):
        peer_loop(lambda d: copy(d, me).start())
        return pltpu.make_async_copy(
            src.at[pl.ds(pl.multiple_of(me * cap, cap), cap), :],
            dst.at[:, pl.ds(pl.multiple_of(me * hd, hd), hd)],
            local_sem.at[sem],
        )

    peer_loop(lambda d: copy_b(d, d).wait_recv())
    v_all = recv_b[...].reshape(total, hd)
    for rb in range(blocks):
        end = (rb + 1) * rows
        out_o[rb * rows : end, :] = jnp.dot(
            lows[rb], v_all[:end], preferred_element_type=F32
        ).astype(BF16)
    own_o = finish(copy_o, out_o, attn_in, 13)
    own_o.start()

    peer_loop(lambda d: copy_c(d, d).wait_recv())
    u_all = recv_c[...].reshape(total, hd)

    def column_sums(left, right):
        tiles = [None] * blocks
        for rb in range(blocks):
            end = (rb + 1) * rows
            got = lax.dot_general(
                left[rb], right[rb * rows : end], TN, preferred_element_type=F32
            )
            for kb in range(rb + 1):
                tile = got[kb * rows : (kb + 1) * rows]
                tiles[kb] = tile if tiles[kb] is None else tiles[kb] + tile
        return tiles

    for kb, tile in enumerate(column_sums(lows, u_all)):
        out_v[kb * rows : (kb + 1) * rows, :] = tile.astype(BF16)
    own_v = finish(copy_v, out_v, dv_hbm.at[0], 12)
    own_v.start()

    lowered = []
    dm = jnp.zeros((1, 1), F32)
    for rb in range(blocks):
        end = (rb + 1) * rows
        grad_probs = lax.dot_general(
            u_all[rb * rows : end], v_all[:end], NT, preferred_element_type=F32
        )
        inner = jnp.sum(probs[rb] * grad_probs, axis=1, keepdims=True)
        grad_score = probs[rb] * (grad_probs - inner)
        by_row = jnp.sum(grad_score * plains[rb], axis=1, keepdims=True)
        dm = dm + jnp.sum(by_row, axis=0, keepdims=True)
        low = (grad_score * (temp * scale)).astype(BF16)
        lowered.append(low)
        out_q[rb * rows : end, :] = jnp.dot(
            low, k_all[:end], preferred_element_type=F32
        ).astype(BF16)
    own_q = finish(copy_q, out_q, dq_hbm.at[0], 10)
    own_q.start()
    for kb, tile in enumerate(column_sums(lowered, q_all)):
        out_k[kb * rows : (kb + 1) * rows, :] = tile.astype(BF16)
    own_k = finish(copy_k, out_k, dk_hbm.at[0], 11)
    own_k.start()

    dm_all[my_rep] = jnp.broadcast_to(dm, (8, 128))

    def copy_dm(r, slot):
        return pltpu.make_async_remote_copy(
            src_ref=dm_all.at[slot],
            dst_ref=dm_all.at[slot],
            send_sem=dm_send.at[r],
            recv_sem=dm_recv.at[slot],
            device_id={"rep": r},
            device_id_type=MESH,
        )

    for r in range(1, reps):
        copy_dm(lax.rem(my_rep + r, reps), my_rep).start()

    stores = [
        local_copy(a, b, 7 + i)
        for i, (a, b) in enumerate(
            (
                (mixed_ref, mixed_hbm),
                (gg_ref, gg_hbm),
                (dm_ref, dm_hbm),
            )
        )
    ]
    own_o.wait()
    for copy in (copy_a, copy_b, copy_c):
        peer_loop(lambda d: copy(d, me).wait_send())
    peer_loop(lambda d: copy_o(d, d).wait_recv())
    attn = attn_in[...].astype(F32)
    mixed_ref[0] = (gate * attn).astype(BF16)
    dots = jnp.sum(cot_in[...].astype(F32) * attn, axis=1, keepdims=True)
    grad_gate = jnp.where(live, sig * (1.0 - sig) * dots, 0.0)
    diagonal = lax.broadcasted_iota(jnp.int32, (cap, cap), 0) == lax.broadcasted_iota(
        jnp.int32, (cap, cap), 1
    )
    gg_ref[...] = jnp.sum(jnp.where(diagonal, grad_gate, 0.0), axis=0, keepdims=True)
    stores[0].start()
    stores[1].start()

    peer_loop(lambda d: copy_o(d, me).wait_send())
    for copy in (copy_v, copy_q):
        peer_loop(lambda d: copy(d, d).wait_recv())
    for r in range(1, reps):
        other = lax.rem(my_rep + r, reps)
        copy_dm(other, other).wait_recv()
    summed = dm_all[0]
    for r in range(1, reps):
        summed = summed + dm_all[r]
    dm_ref[...] = summed[0:1, 0:1]

    stores[2].start()
    for copy in (copy_v, copy_q):
        peer_loop(lambda d: copy(d, me).wait_send())
    for r in range(1, reps):
        copy_dm(lax.rem(my_rep + r, reps), my_rep).wait_send()
    for c in stores + [own_v, own_q, own_k]:
        c.wait()
    peer_loop(lambda d: copy_k(d, d).wait_recv())
    peer_loop(lambda d: copy_k(d, me).wait_send())


def store(*refs):
    ins, outs, held, got, put = refs[:6], refs[6:12], refs[12:18], refs[18], refs[19]
    reads = [pltpu.make_async_copy(ins[i], held[i], got.at[i]) for i in range(6)]
    writes = [pltpu.make_async_copy(held[i], outs[i], put.at[i]) for i in range(6)]
    for c in reads:
        c.start()
    for r, w in zip(reads, writes):
        r.wait()
        w.start()
    for c in writes:
        c.wait()


def local(n, reps, q, k, v, levels, logits, mult, cot):
    tokens, width = q.shape[1], q.shape[2]
    cap = cot.shape[1]
    hd = width // mult.shape[0]
    total = n * cap
    far = pl.BlockSpec(memory_space=pltpu.HBM)
    wide = jax.ShapeDtypeStruct((1, cap, width), BF16)
    outs = pl.pallas_call(
        functools.partial(kernel, n, reps, cap, hd),
        out_shape=(
            wide,
            jax.ShapeDtypeStruct((1, cap), F32),
            wide,
            wide,
            wide,
            jax.ShapeDtypeStruct((1, 1), F32),
        ),
        in_specs=[far] * 7,
        out_specs=(far,) * 6,
        scratch_shapes=[
            pltpu.VMEM((1, cap, width), BF16),
            pltpu.VMEM((1, cap), F32),
            pltpu.VMEM((1, cap, width), BF16),
            pltpu.VMEM((1, cap, width), BF16),
            pltpu.VMEM((1, cap, width), BF16),
            pltpu.VMEM((1, 1), F32),
            pltpu.VMEM((tokens, width), BF16),
            pltpu.VMEM((tokens, width), BF16),
            pltpu.VMEM((tokens, width), BF16),
            pltpu.VMEM((cap, width), BF16),
            pltpu.VMEM((1, tokens), jnp.int32),
            pltpu.VMEM((1, tokens), F32),
            pltpu.VMEM((1, n), F32),
            pltpu.VMEM((n, 2 * cap + 16, hd), BF16),
            pltpu.VMEM((n, cap, hd), BF16),
            pltpu.VMEM((n, cap, hd), BF16),
            pltpu.VMEM((n, 2 * cap + 16, hd), BF16),
            pltpu.VMEM((n, cap, hd), BF16),
            pltpu.VMEM((n, cap, hd), BF16),
            pltpu.VMEM((total, hd), BF16),
            pltpu.VMEM((total, hd), BF16),
            pltpu.VMEM((total, hd), BF16),
            pltpu.VMEM((total, hd), BF16),
            pltpu.VMEM((cap, width), BF16),
            pltpu.VMEM((reps, 8, 128), F32),
            pltpu.SemaphoreType.DMA((14,)),
            pltpu.SemaphoreType.DMA((7, n)),
            pltpu.SemaphoreType.DMA((7, n)),
            pltpu.SemaphoreType.DMA((reps,)),
            pltpu.SemaphoreType.DMA((reps,)),
        ],
        compiler_params=pltpu.CompilerParams(
            collective_id=0, has_side_effects=True, vmem_limit_bytes=56 * 1024 * 1024
        ),
    )(q, k, v, levels, logits, mult.reshape(1, n), cot)
    mixed, gg, dq, dk, dv, dm = pl.pallas_call(
        store,
        out_shape=tuple(jax.ShapeDtypeStruct(o.shape, o.dtype) for o in outs),
        in_specs=[far] * 6,
        out_specs=(far,) * 6,
        scratch_shapes=[pltpu.VMEM(o.shape, o.dtype) for o in outs]
        + [pltpu.SemaphoreType.DMA((6,)), pltpu.SemaphoreType.DMA((6,))],
        compiler_params=pltpu.CompilerParams(vmem_limit_bytes=56 * 1024 * 1024),
    )(*outs)
    return mixed, gg, dq, dk, dv, dm[0]


def solution(mesh):
    n, reps = mesh.shape["seq"], mesh.shape["rep"]
    in_specs = (
        P("rep", "seq", None),
        P("rep", "seq", None),
        P("rep", "seq", None),
        P("rep", "seq"),
        P("rep", "seq"),
        P(),
        P("rep", "seq", None),
    )
    out_specs = (
        P("rep", "seq", None),
        P("rep", "seq"),
        P("rep", "seq", None),
        P("rep", "seq", None),
        P("rep", "seq", None),
        P("seq"),
    )
    return jax.shard_map(
        functools.partial(local, n, reps),
        mesh=mesh,
        in_specs=in_specs,
        out_specs=out_specs,
        check_vma=False,
    )
```

```python
import functools
import math

import jax
import jax.numpy as jnp
from jax import lax
from jax.experimental import pallas as pl
from jax.experimental.pallas import tpu as pltpu
from jax.sharding import PartitionSpec as P

STEP = 2
MESH = pl.DeviceIdType.MESH
BF16 = jnp.bfloat16
F32 = jnp.float32


def kernel(
    n,
    reps,
    cap,
    hd,
    q_hbm,
    k_hbm,
    v_hbm,
    lev_hbm,
    logit_hbm,
    mult_hbm,
    cot_hbm,
    mixed_hbm,
    gg_hbm,
    dq_hbm,
    dk_hbm,
    dv_hbm,
    dm_hbm,
    mixed_ref,
    gg_ref,
    dq_ref,
    dk_ref,
    dv_ref,
    dm_ref,
    q_in,
    k_in,
    v_in,
    cot_in,
    lev_in,
    logit_in,
    mult_in,
    send_a,
    send_b,
    send_c,
    recv_a,
    recv_b,
    recv_c,
    out_o,
    out_q,
    out_k,
    out_v,
    attn_in,
    dm_all,
    local_sem,
    send_sem,
    recv_sem,
    dm_send,
    dm_recv,
):
    me = lax.axis_index("seq")
    my_rep = lax.axis_index("rep")
    total = n * cap
    scale = 1.0 / math.sqrt(hd)

    def local_copy(src, dst, s):
        return pltpu.make_async_copy(src, dst, local_sem.at[s])

    lev_copy = local_copy(lev_hbm, lev_in, 0)
    logit_copy = local_copy(logit_hbm, logit_in, 1)
    q_copy = local_copy(q_hbm.at[0], q_in, 2)
    k_copy = local_copy(k_hbm.at[0], k_in, 3)
    v_copy = local_copy(v_hbm.at[0], v_in, 4)
    cot_copy = local_copy(cot_hbm.at[0], cot_in, 5)
    mult_copy = local_copy(mult_hbm, mult_in, 6)
    for c in (lev_copy, q_copy, k_copy, v_copy, logit_copy, cot_copy, mult_copy):
        c.start()

    def peer_loop(f):
        if n <= 8:
            for step in range(1, n):
                f(lax.rem(me + step, n))
        else:

            def body(step, carry):
                f(lax.rem(me + step, n))
                return carry

            lax.fori_loop(1, n, body, 0)

    barrier = pltpu.get_barrier_semaphore()
    peer_loop(
        lambda d: pl.semaphore_signal(
            barrier, inc=1, device_id={"seq": d}, device_id_type=MESH
        )
    )
    for r in range(1, reps):
        pl.semaphore_signal(
            barrier,
            inc=1,
            device_id={"rep": lax.rem(my_rep + r, reps)},
            device_id_type=MESH,
        )

    lev_copy.wait()
    tokens = lev_in.shape[1]
    active = lev_in[...] > STEP
    flags = jnp.where(active, 1.0, 0.0)
    upto = jnp.where(
        lax.broadcasted_iota(jnp.int32, (tokens, tokens), 0)
        <= lax.broadcasted_iota(jnp.int32, (tokens, tokens), 1),
        1.0,
        0.0,
    ).astype(BF16)
    ranked = jnp.dot(
        jnp.broadcast_to(flags, (16, tokens)).astype(BF16), upto, preferred_element_type=F32
    )[0:1] - 1.0
    slot_ids = lax.broadcasted_iota(jnp.int32, (cap, tokens), 0).astype(F32)
    matched = (ranked == slot_ids) & active
    chosen = jnp.where(matched, 1.0, 0.0)
    pick = chosen.astype(BF16)
    live = jnp.sum(chosen, axis=1, keepdims=True) > 0.5
    count = jnp.sum(flags, axis=1, keepdims=True)

    for h in range(n):
        send_a[h, 2 * cap :, :] = jnp.broadcast_to(count, (16, hd)).astype(BF16)

    def gather(src, dst, row):
        for c in range(0, n, 2):
            part = jnp.dot(
                pick, src[:, c * hd : (c + 2) * hd], preferred_element_type=F32
            ).astype(BF16)
            dst[c, row : row + cap, :] = part[:, :hd]
            dst[c + 1, row : row + cap, :] = part[:, hd:]

    def to_head(part, src, dst, low, high):
        def copy(d, slot):
            return pltpu.make_async_remote_copy(
                src_ref=src.at[d, low:high, :],
                dst_ref=dst.at[slot, low:high, :],
                send_sem=send_sem.at[part, d],
                recv_sem=recv_sem.at[part, slot],
                device_id={"seq": d},
                device_id_type=MESH,
            )

        return copy

    copy_a = to_head(0, send_a, recv_a, cap, 2 * cap + 16)
    copy_b = to_head(1, send_b, recv_b, 0, cap)
    copy_c = to_head(2, send_c, recv_c, 0, cap)
    copy_d = to_head(7, send_a, recv_a, 0, cap)

    q_copy.wait()
    gather(q_in, send_a, 0)
    pl.semaphore_wait(barrier, n - 1 + reps - 1)
    peer_loop(lambda d: copy_d(d, me).start())
    k_copy.wait()
    gather(k_in, send_a, cap)
    peer_loop(lambda d: copy_a(d, me).start())
    recv_a[me] = send_a[me]

    v_copy.wait()
    gather(v_in, send_b, 0)
    peer_loop(lambda d: copy_b(d, me).start())
    recv_b[me] = send_b[me]

    logit_copy.wait()
    logits = jnp.sum(jnp.where(matched, logit_in[...], 0.0), axis=1, keepdims=True)
    sig = jax.nn.sigmoid(logits)
    gate = jnp.where(live, sig, 0.0)
    cot_copy.wait()
    for h in range(n):
        send_c[h] = (gate * cot_in[:, h * hd : (h + 1) * hd].astype(F32)).astype(BF16)
    peer_loop(lambda d: copy_c(d, me).start())
    recv_c[me] = send_c[me]

    mult_copy.wait()
    heads = lax.broadcasted_iota(jnp.int32, mult_in.shape, 1)
    temp = jnp.sum(jnp.where(heads == me, mult_in[...], 0.0), axis=1, keepdims=True)
    peer_loop(lambda d: copy_d(d, d).wait_recv())
    peer_loop(lambda d: copy_a(d, d).wait_recv())
    q_all = recv_a[:, 0:cap, :].reshape(total, hd)
    k_all = recv_a[:, cap : 2 * cap, :].reshape(total, hd)
    rows = min(total, 128)
    blocks = total // rows
    lane = lax.broadcasted_iota(jnp.int32, (1, hd), 1)
    per = hd // cap
    pieces = []
    for c in range(total // hd):
        counts = jnp.zeros((1, hd), F32)
        for b in range(per):
            got = recv_a[c * per + b, 2 * cap :, :].astype(F32)[0:1]
            counts = jnp.where(lane // cap == b, got, counts)
        pieces.append(jnp.where((lane % cap).astype(F32) < counts, 1.0, 0.0))
    live_keys = jnp.concatenate(pieces, axis=1) > 0.5

    NT = (((1,), (1,)), ((), ()))
    TN = (((0,), (0,)), ((), ()))
    plains, probs, lows = [], [], []
    for rb in range(blocks):
        end = (rb + 1) * rows
        plain = (
            lax.dot_general(
                q_all[rb * rows : end], k_all[:end], NT, preferred_element_type=F32
            )
            * scale
        )
        row_id = lax.broadcasted_iota(jnp.int32, (rows, end), 0) + rb * rows
        col_id = lax.broadcasted_iota(jnp.int32, (rows, end), 1)
        allowed = (col_id <= row_id) & live_keys[:, :end]
        scores = jnp.where(allowed, temp * plain, -jnp.inf)
        top = jnp.max(scores, axis=1, keepdims=True)
        shifted = jnp.exp(scores - top)
        prob = shifted * (1.0 / jnp.sum(shifted, axis=1, keepdims=True))
        plains.append(plain)
        probs.append(prob)
        lows.append(prob.astype(BF16))

    def to_slots(part, src, dst):
        def copy(d, slot):
            return pltpu.make_async_remote_copy(
                src_ref=src.at[pl.ds(pl.multiple_of(d * cap, cap), cap), :],
                dst_ref=dst.at[:, pl.ds(pl.multiple_of(slot * hd, hd), hd)],
                send_sem=send_sem.at[part, d],
                recv_sem=recv_sem.at[part, slot],
                device_id={"seq": d},
                device_id_type=MESH,
            )

        return copy

    copy_o = to_slots(3, out_o, attn_in)
    copy_v = to_slots(4, out_v, dv_hbm.at[0])
    copy_q = to_slots(5, out_q, dq_hbm.at[0])
    copy_k = to_slots(6, out_k, dk_hbm.at[0])

    def finish(copy, src, dst, sem):
        peer_loop(lambda d: copy(d, me).start())
        return pltpu.make_async_copy(
            src.at[pl.ds(pl.multiple_of(me * cap, cap), cap), :],
            dst.at[:, pl.ds(pl.multiple_of(me * hd, hd), hd)],
            local_sem.at[sem],
        )

    peer_loop(lambda d: copy_b(d, d).wait_recv())
    v_all = recv_b[...].reshape(total, hd)
    for rb in range(blocks):
        end = (rb + 1) * rows
        out_o[rb * rows : end, :] = jnp.dot(
            lows[rb], v_all[:end], preferred_element_type=F32
        ).astype(BF16)
    own_o = finish(copy_o, out_o, attn_in, 13)
    own_o.start()

    peer_loop(lambda d: copy_c(d, d).wait_recv())
    u_all = recv_c[...].reshape(total, hd)

    def column_sums(left, right):
        tiles = [None] * blocks
        for rb in range(blocks):
            end = (rb + 1) * rows
            got = lax.dot_general(
                left[rb], right[rb * rows : end], TN, preferred_element_type=F32
            )
            for kb in range(rb + 1):
                tile = got[kb * rows : (kb + 1) * rows]
                tiles[kb] = tile if tiles[kb] is None else tiles[kb] + tile
        return tiles

    for kb, tile in enumerate(column_sums(lows, u_all)):
        out_v[kb * rows : (kb + 1) * rows, :] = tile.astype(BF16)
    own_v = finish(copy_v, out_v, dv_hbm.at[0], 12)
    own_v.start()

    lowered = []
    dm = jnp.zeros((1, 1), F32)
    for rb in range(blocks):
        end = (rb + 1) * rows
        grad_probs = lax.dot_general(
            u_all[rb * rows : end], v_all[:end], NT, preferred_element_type=F32
        )
        inner = jnp.sum(probs[rb] * grad_probs, axis=1, keepdims=True)
        grad_score = probs[rb] * (grad_probs - inner)
        by_row = jnp.sum(grad_score * plains[rb], axis=1, keepdims=True)
        dm = dm + jnp.sum(by_row, axis=0, keepdims=True)
        low = (grad_score * (temp * scale)).astype(BF16)
        lowered.append(low)
        out_q[rb * rows : end, :] = jnp.dot(
            low, k_all[:end], preferred_element_type=F32
        ).astype(BF16)
    own_q = finish(copy_q, out_q, dq_hbm.at[0], 10)
    own_q.start()
    for kb, tile in enumerate(column_sums(lowered, q_all)):
        out_k[kb * rows : (kb + 1) * rows, :] = tile.astype(BF16)
    own_k = finish(copy_k, out_k, dk_hbm.at[0], 11)
    own_k.start()

    dm_all[my_rep] = jnp.broadcast_to(dm, (8, 128))

    def copy_dm(r, slot):
        return pltpu.make_async_remote_copy(
            src_ref=dm_all.at[slot],
            dst_ref=dm_all.at[slot],
            send_sem=dm_send.at[r],
            recv_sem=dm_recv.at[slot],
            device_id={"rep": r},
            device_id_type=MESH,
        )

    for r in range(1, reps):
        copy_dm(lax.rem(my_rep + r, reps), my_rep).start()

    stores = [
        local_copy(a, b, 7 + i)
        for i, (a, b) in enumerate(
            (
                (mixed_ref, mixed_hbm),
                (gg_ref, gg_hbm),
                (dm_ref, dm_hbm),
            )
        )
    ]
    own_o.wait()
    peer_loop(lambda d: copy_o(d, d).wait_recv())
    attn = attn_in[...].astype(F32)
    mixed_ref[0] = (gate * attn).astype(BF16)
    dots = jnp.sum(cot_in[...].astype(F32) * attn, axis=1, keepdims=True)
    grad_gate = jnp.where(live, sig * (1.0 - sig) * dots, 0.0)
    diagonal = lax.broadcasted_iota(jnp.int32, (cap, cap), 0) == lax.broadcasted_iota(
        jnp.int32, (cap, cap), 1
    )
    gg_ref[...] = jnp.sum(jnp.where(diagonal, grad_gate, 0.0), axis=0, keepdims=True)
    stores[0].start()
    stores[1].start()

    for copy in (copy_v, copy_q):
        peer_loop(lambda d: copy(d, d).wait_recv())
    for r in range(1, reps):
        other = lax.rem(my_rep + r, reps)
        copy_dm(other, other).wait_recv()
    summed = dm_all[0]
    for r in range(1, reps):
        summed = summed + dm_all[r]
    dm_ref[...] = summed[0:1, 0:1]

    stores[2].start()
    peer_loop(lambda d: copy_k(d, d).wait_recv())
    for copy in (copy_d, copy_a, copy_b, copy_c, copy_o, copy_v, copy_q, copy_k):
        peer_loop(lambda d: copy(d, me).wait_send())
    for r in range(1, reps):
        copy_dm(lax.rem(my_rep + r, reps), my_rep).wait_send()
    for c in stores + [own_v, own_q, own_k]:
        c.wait()


def store(*refs):
    ins, outs, held, got, put = refs[:6], refs[6:12], refs[12:18], refs[18], refs[19]
    reads = [pltpu.make_async_copy(ins[i], held[i], got.at[i]) for i in range(6)]
    writes = [pltpu.make_async_copy(held[i], outs[i], put.at[i]) for i in range(6)]
    for c in reads:
        c.start()
    for r, w in zip(reads, writes):
        r.wait()
        w.start()
    for c in writes:
        c.wait()


def local(n, reps, q, k, v, levels, logits, mult, cot):
    tokens, width = q.shape[1], q.shape[2]
    cap = cot.shape[1]
    hd = width // mult.shape[0]
    total = n * cap
    far = pl.BlockSpec(memory_space=pltpu.HBM)
    wide = jax.ShapeDtypeStruct((1, cap, width), BF16)
    outs = pl.pallas_call(
        functools.partial(kernel, n, reps, cap, hd),
        out_shape=(
            wide,
            jax.ShapeDtypeStruct((1, cap), F32),
            wide,
            wide,
            wide,
            jax.ShapeDtypeStruct((1, 1), F32),
        ),
        in_specs=[far] * 7,
        out_specs=(far,) * 6,
        scratch_shapes=[
            pltpu.VMEM((1, cap, width), BF16),
            pltpu.VMEM((1, cap), F32),
            pltpu.VMEM((1, cap, width), BF16),
            pltpu.VMEM((1, cap, width), BF16),
            pltpu.VMEM((1, cap, width), BF16),
            pltpu.VMEM((1, 1), F32),
            pltpu.VMEM((tokens, width), BF16),
            pltpu.VMEM((tokens, width), BF16),
            pltpu.VMEM((tokens, width), BF16),
            pltpu.VMEM((cap, width), BF16),
            pltpu.VMEM((1, tokens), jnp.int32),
            pltpu.VMEM((1, tokens), F32),
            pltpu.VMEM((1, n), F32),
            pltpu.VMEM((n, 2 * cap + 16, hd), BF16),
            pltpu.VMEM((n, cap, hd), BF16),
            pltpu.VMEM((n, cap, hd), BF16),
            pltpu.VMEM((n, 2 * cap + 16, hd), BF16),
            pltpu.VMEM((n, cap, hd), BF16),
            pltpu.VMEM((n, cap, hd), BF16),
            pltpu.VMEM((total, hd), BF16),
            pltpu.VMEM((total, hd), BF16),
            pltpu.VMEM((total, hd), BF16),
            pltpu.VMEM((total, hd), BF16),
            pltpu.VMEM((cap, width), BF16),
            pltpu.VMEM((reps, 8, 128), F32),
            pltpu.SemaphoreType.DMA((14,)),
            pltpu.SemaphoreType.DMA((8, n)),
            pltpu.SemaphoreType.DMA((8, n)),
            pltpu.SemaphoreType.DMA((reps,)),
            pltpu.SemaphoreType.DMA((reps,)),
        ],
        compiler_params=pltpu.CompilerParams(
            collective_id=0, has_side_effects=True, vmem_limit_bytes=56 * 1024 * 1024
        ),
    )(q, k, v, levels, logits, mult.reshape(1, n), cot)
    mixed, gg, dq, dk, dv, dm = pl.pallas_call(
        store,
        out_shape=tuple(jax.ShapeDtypeStruct(o.shape, o.dtype) for o in outs),
        in_specs=[far] * 6,
        out_specs=(far,) * 6,
        scratch_shapes=[pltpu.VMEM(o.shape, o.dtype) for o in outs]
        + [pltpu.SemaphoreType.DMA((6,)), pltpu.SemaphoreType.DMA((6,))],
        compiler_params=pltpu.CompilerParams(vmem_limit_bytes=56 * 1024 * 1024),
    )(*outs)
    return mixed, gg, dq, dk, dv, dm[0]


def solution(mesh):
    n, reps = mesh.shape["seq"], mesh.shape["rep"]
    in_specs = (
        P("rep", "seq", None),
        P("rep", "seq", None),
        P("rep", "seq", None),
        P("rep", "seq"),
        P("rep", "seq"),
        P(),
        P("rep", "seq", None),
    )
    out_specs = (
        P("rep", "seq", None),
        P("rep", "seq"),
        P("rep", "seq", None),
        P("rep", "seq", None),
        P("rep", "seq", None),
        P("seq"),
    )
    return jax.shard_map(
        functools.partial(local, n, reps),
        mesh=mesh,
        in_specs=in_specs,
        out_specs=out_specs,
        check_vma=False,
    )
```
